256 devices in a mesh: row: 8 (over x, z_hi), col: 32 (over z_lo, y, core).
Axes of the slice: x: 4, y: 4, z: 8 (z_hi: 2, z_lo: 4; z = z_hi * 4 + z_lo), core: 2. Of those that a mesh axis runs over, the one named last changes fastest.
Arguments:
- activations: bfloat16 [3072, 8192], P(None, 'row'), may hold values from -6 to 6
- out_grads: bfloat16 [3072, 8192], P(None, 'col'), may hold values from -6 to 6
- act_basis: bfloat16 [8192, 8192], P('row', 'col'), may hold values from -0.0625 to 0.0625
- grad_basis: bfloat16 [8192, 8192], P('col', 'row'), may hold values from -0.0625 to 0.0625
Outputs:
- eigen_diag: float32 [8192, 8192], P('row', 'col')
The draws below stay inside these ranges and needn't reach their ends.
All inputs are finite; a program needn't handle non-finite values.
Results may differ from the reference program's by a relative error of at most 0.0029.
Values may be sent and summed in bfloat16 or wider, within the bound.
No kernel may reach another device: no remote copies, remote signals or barrier semaphores. Data moves between devices by JAX's collectives and lax.ppermute only.
A program may use at most 64 MiB of HBM per device.

```python
import jax
import jax.numpy as jnp
from jax import lax

D = 8192
SEQS = 6
LEN = 512
TOKENS = 3072


def level_of(own_key, dims, shards, low, top_value):
    factor_of = 1.0
    for position, blocks in shards:
        steps = jax.random.uniform(jax.random.fold_in(jax.random.fold_in(own_key, 6), position), (blocks,), jnp.float32, low / len(shards), top_value / len(shards))
        factor_of = factor_of * jnp.repeat(jnp.exp(steps), dims[position] // blocks).reshape((-1,) + (1,) * (len(dims) - 1 - position))
    return factor_of


def gaussian(own_key, extent, spread, bound, split=(), held_as=jnp.bfloat16):
    loudness = level_of(own_key, extent, split, -0.22, 0.18) if split else 1.0
    array = jax.random.normal(own_key, extent, jnp.float32) * spread * loudness
    return jnp.minimum(jnp.maximum(array, -bound), bound).astype(held_as)


def setup_inputs(seed: int = 0) -> dict:
    seeds = jax.random.split(jax.random.key(seed), 5)
    return {
        "activations": gaussian(seeds[0], (TOKENS, D), 1.0, 6.0, ((1, 8),)),
        "out_grads": gaussian(seeds[1], (TOKENS, D), 1.0, 6.0, ((1, 32),)),
        "act_basis": gaussian(seeds[2], (D, D), D ** -0.5, 0.0625, ((0, 8), (1, 32))),
        "grad_basis": gaussian(seeds[3], (D, D), D ** -0.5, 0.0625, ((0, 32), (1, 8))),
    }


def reference(activations, out_grads, act_basis, grad_basis):
    act_rot = jnp.dot(activations, act_basis, preferred_element_type=jnp.float32).astype(jnp.bfloat16)
    grad_rot = jnp.dot(out_grads, grad_basis, preferred_element_type=jnp.float32).astype(jnp.bfloat16)
    scale = 1.0 / jnp.sqrt(jnp.float32(LEN))

    def add_sequence(total, pair):
        rotated = jnp.dot(pair[0].T, pair[1], preferred_element_type=jnp.float32) * scale
        return (total + rotated * rotated, None)
    total, unused = lax.scan(add_sequence, jnp.zeros((D, D), jnp.float32), (grad_rot.reshape(SEQS, LEN, D), act_rot.reshape(SEQS, LEN, D)))
    return total / jnp.float32(SEQS)
```

```python
import jax
import jax.numpy as jnp
from jax import lax
from jax.sharding import PartitionSpec as P

LEN = 512
F32, BF16, F16 = jnp.float32, jnp.bfloat16, jnp.float16
PAIRS = 2


def col_swap(a, y_xor=0, z_xor=0, core_xor=0):
    perm = [(i, i ^ (z_xor * 8 + y_xor * 2 + core_xor)) for i in range(32)]
    return lax.ppermute(a, "col", perm)


def row_swap(a, x_xor=0, z_xor=0):
    perm = [(i, i ^ (x_xor * 2 + z_xor)) for i in range(8)]
    return lax.ppermute(a, "row", perm)


def exponent(bound):
    return jnp.maximum(jnp.floor(jnp.log2(bound)) + 2.0, -100.0)


def encode(part, bound):
    e = exponent(bound)
    flat = part.reshape(-1, part.shape[-1])
    body = (flat * jnp.exp2(15.0 - e)).astype(F16)
    return jnp.concatenate([body, jnp.full((16, flat.shape[1]), e, F32).astype(F16)], 0)


def decode(sent, shape):
    e = sent[-16, 0].astype(F32)
    part = sent[:-16].astype(F32).reshape(shape) * jnp.exp2(e - 15.0)
    return part, jnp.exp2(e - 1.0)


def top(a):
    return jnp.max(jnp.abs(a)).astype(F32)


def take(a, axis, index):
    return lax.dynamic_index_in_dim(a, index, axis, keepdims=False)


def xor_order(a, axis, v):
    shape = a.shape
    a = a.reshape(shape[:axis] + (2, 2) + shape[axis + 1 :])
    a = jnp.where((v & 2) != 0, jnp.flip(a, axis), a)
    a = jnp.where((v & 1) != 0, jnp.flip(a, axis + 1), a)
    return a.reshape(shape)


def shards(activations, out_grads, act_basis, grad_basis):
    row, col = lax.axis_index("row"), lax.axis_index("col")
    x = row // 2
    zl, y, core = col // 8, (col // 2) % 4, col % 2
    tokens = activations.shape[0]
    half = tokens // 2
    seqs = half // LEN
    dirs, cols = grad_basis.shape[1], 2 * act_basis.shape[1]
    quarter, piece = LEN // 4, LEN // 16
    scale = 1.0 / jnp.sqrt(F32(LEN))

    og_away = lax.dynamic_slice_in_dim(out_grads, (1 - core) * half, half, 0)
    og_own = lax.dynamic_slice_in_dim(out_grads, core * half, half, 0)
    og = jnp.concatenate([og_own, col_swap(og_away, core_xor=1)], 1)
    gb = jnp.concatenate([grad_basis, col_swap(grad_basis, core_xor=1)], 0)
    ab = jnp.concatenate([act_basis, col_swap(act_basis, core_xor=1)], 1)
    acts = lax.dynamic_slice_in_dim(activations, core * half, half, 0)

    a_bound = acts.shape[1] * top(acts) * top(ab)
    a_part = jnp.dot(acts, ab, preferred_element_type=F32).reshape(seqs, 4, quarter, cols)
    a_sum = take(a_part, 1, x)
    a_sent = [row_swap(encode(take(a_part, 1, x ^ k), a_bound), x_xor=k) for k in (1, 2, 3)]
    a_top = a_bound
    for sent in a_sent:
        part, bound = decode(sent, a_sum.shape)
        a_sum, a_top = a_sum + part, a_top + bound
    part, _ = decode(row_swap(encode(a_sum, a_top), z_xor=1), a_sum.shape)
    a_own = (a_sum + part).astype(BF16)
    a_all = jnp.stack([a_own] + [row_swap(a_own, x_xor=k) for k in (1, 2, 3)])
    a_all = a_all.reshape(4, seqs, 4, piece, cols)
    a_all = xor_order(xor_order(a_all, 0, x ^ y), 2, zl)
    a_all = a_all.transpose(1, 0, 2, 3, 4).reshape(seqs, LEN, cols)

    g_bound = og.shape[1] * top(og) * top(gb)
    g_part = jnp.dot(og, gb, preferred_element_type=F32).reshape(seqs, 4, quarter, dirs)
    width = dirs // (2 * PAIRS)
    outs = []
    for pair in range(PAIRS):
        sums, bounds = [], []
        for kind, (first, second) in enumerate(((1, 3), (3, 1))):
            at = (2 * pair + kind) * width
            block = g_part[..., at : at + width]
            away = jnp.stack([take(block, 1, y ^ first), take(block, 1, y ^ 2)])
            keep = jnp.stack([take(block, 1, y), take(block, 1, y ^ second)])
            part, bound = decode(col_swap(encode(away, g_bound), y_xor=first), keep.shape)
            keep, bound = keep + part, g_bound + bound
            part, more = decode(col_swap(encode(keep[1], bound), y_xor=second), keep.shape[1:])
            sums.append(keep[0] + part)
            bounds.append(bound + more)
        bound = jnp.maximum(*bounds)
        g_sum = jnp.concatenate(sums, 2).reshape(seqs, 4, piece, 2 * width)
        total = take(g_sum, 1, zl)
        for k in (1, 2, 3):
            sent = col_swap(encode(take(g_sum, 1, zl ^ k), bound), z_xor=k)
            total = total + decode(sent, total.shape)[0]
        g_own = total.astype(BF16)
        g_quarter = jnp.stack([g_own] + [col_swap(g_own, z_xor=k) for k in (1, 2, 3)])
        for kind, (first, second) in enumerate(((1, 3), (3, 1))):
            own = g_quarter[..., kind * width : (kind + 1) * width]
            near = jnp.stack([own, col_swap(own, y_xor=first)])
            far = col_swap(near, y_xor=second)
            order = [near[0], near[1], far[1], far[0]] if first == 1 else [near[0], far[0], far[1], near[1]]
            g_all = jnp.stack(order).transpose(2, 0, 1, 3, 4).reshape(seqs, LEN, width)
            total = jnp.zeros((width, cols), F32)
            for s in range(seqs):
                r = lax.dot_general(g_all[s], a_all[s], (((0,), (0,)), ((), ())), preferred_element_type=F32) * scale
                total = total + r * r
            outs.append(total)
    out = jnp.concatenate(outs, 0)
    other = col_swap(out[:, cols // 2 :], core_xor=1)
    return (out[:, : cols // 2] + other) / F32(2 * seqs)


def solution(mesh):
    return jax.shard_map(
        shards,
        mesh=mesh,
        in_specs=(P(None, "row"), P(None, "col"), P("row", "col"), P("col", "row")),
        out_specs=P("row", "col"),
        check_vma=False,
    )
```

```python
import functools

import jax
import jax.numpy as jnp
from jax import lax
from jax.experimental import pallas as pl
from jax.experimental.pallas import tpu as pltpu
from jax.sharding import PartitionSpec as P

LEN = 512
SEQS, HALF, QUARTER, PIECE, STEP = 3, 1536, 384, 96, 32
TAIL = 16
PAIRS = 2
F32, BF16 = jnp.float32, jnp.bfloat16


def col_swap(a, y=0, z=0, core=0):
    perm = [(i, i ^ (z * 8 + y * 2 + core)) for i in range(32)]
    return lax.ppermute(a, "col", perm)


def row_swap(a, x=0, z=0):
    perm = [(i, i ^ (x * 2 + z)) for i in range(8)]
    return lax.ppermute(a, "row", perm)


def exponent(v):
    return jnp.maximum(jnp.floor(jnp.log2(jnp.max(jnp.abs(v), keepdims=True))) + 2.0, -100.0)


def put(ref, v):
    rows = v.shape[0]
    e = exponent(v)
    t = v * jnp.exp2(16.0 - e)
    t = t * t
    t = t * t
    t = t * t
    ref[0:rows, :] = jnp.where(v < 0, -t, t).astype(BF16)
    ref[rows : rows + TAIL, :] = jnp.broadcast_to(e, (TAIL, ref.shape[1])).astype(BF16)


def get(ref, rows=None):
    end = ref.shape[0]
    e = ref[end - TAIL : end, :][0:1, 0:1].astype(F32)
    c = ref[slice(0, end - TAIL) if rows is None else rows, :].astype(F32)
    t = jnp.exp2(jnp.log2(jnp.abs(c)) * 0.125 + (e - 16.0))
    return jnp.where(c < 0, -t, t)


def quarter_rows(ref, q):
    rows = []
    for z in range(4):
        for s in range(SEQS):
            at = pl.multiple_of(s * LEN + q * (4 * STEP) + z * STEP, STEP)
            rows.append(ref[pl.ds(at, STEP), :])
    return jnp.concatenate(rows, 0)


def call(body, place, outs, ins, specs=None, name=None, flops=0, scratch=()):
    specs = specs or {}

    def whole(shape):
        return pl.BlockSpec(shape, lambda i, s: (0,) * len(shape))

    nbytes = sum(a.size * a.dtype.itemsize for a in ins) + sum(
        functools.reduce(lambda a, b: a * b, s, 1) * jnp.dtype(d).itemsize for s, d in outs
    )
    return pl.pallas_call(
        body,
        out_shape=[jax.ShapeDtypeStruct(s, d) for s, d in outs],
        grid_spec=pltpu.PrefetchScalarGridSpec(
            num_scalar_prefetch=1,
            grid=(1,),
            in_specs=[specs.get(i) or whole(a.shape) for i, a in enumerate(ins)],
            out_specs=[whole(s) for s, _ in outs],
            scratch_shapes=scratch,
        ),
        compiler_params=pltpu.CompilerParams(vmem_limit_bytes=24 * 2**20),
        cost_estimate=pl.CostEstimate(flops=flops, bytes_accessed=nbytes, transcendentals=0),
        name=name,
    )(place, *ins)


def grad_dot(own, got, gb_own, gb_got, q):
    p = jnp.dot(quarter_rows(own, q), gb_own[...], preferred_element_type=F32)
    return p + jnp.dot(quarter_rows(got, q), gb_got[...], preferred_element_type=F32)


def grad_first(place, own, got, gb_own, gb_got, send_a, send_b):
    p = grad_dot(own, got, gb_own, gb_got, place[2] ^ 2)
    w = p.shape[1] // (2 * PAIRS)
    for kind, ref in enumerate((send_a, send_b)):
        put(ref, jnp.concatenate([p[:, (2 * i + kind) * w : (2 * i + kind + 1) * w] for i in range(PAIRS)], 1))


def grad_rest(place, own, got, gb_own, gb_got, p1, p3, p0):
    for j, ref in ((1, p1), (3, p3), (0, p0)):
        ref[...] = grad_dot(own, got, gb_own, gb_got, place[2] ^ j)


def grad_second(place, p1, p3, got_a, got_b, send_p, send_q):
    w = got_a.shape[1]
    put(send_p, jnp.concatenate([p1[:, :w] + get(got_a), p1[:, w:]], 1))
    put(send_q, jnp.concatenate([p3[:, :w], p3[:, w:] + get(got_b)], 1))


def grad_z(place, p0, got_p, got_q, send1, send2, send3, keep):
    for k, ref in ((1, send1), (2, send2), (3, send3), (0, keep)):
        rows = pl.ds(pl.multiple_of((place[3] ^ k) * PIECE, STEP), PIECE)
        v = p0[rows, :] + get(got_p, rows) + get(got_q, rows)
        if k:
            put(ref, v)
        else:
            ref[...] = v


def grad_round(place, own, got1, got2, got3, out):
    out[...] = (own[...] + get(got1) + get(got2) + get(got3)).astype(BF16)


def grad_join(place, g0, g1, g2, g3, out):
    w = out.shape[2]
    for k, ref in enumerate((g0, g1, g2, g3)):
        for kind in range(2):
            out[kind, k * PIECE : (k + 1) * PIECE, :] = ref[:, kind * w : (kind + 1) * w]


def act_first(place, acts, ab_own, ab_got, send1, send2, send3, keep):
    for k, ref in ((1, send1), (2, send2), (3, send3), (0, keep)):
        rows = quarter_rows(acts, place[1] ^ k)
        v = jnp.concatenate([jnp.dot(rows, ab[...], preferred_element_type=F32) for ab in (ab_own, ab_got)], 1)
        if k:
            put(ref, v)
        else:
            ref[...] = v


def act_second(place, keep, got1, got2, got3, send, total):
    v = keep[...]
    for ref in (got1, got2, got3):
        v = v + get(ref)
    total[...] = v
    put(send, v)


def act_round(place, total, got, out):
    out[...] = (total[...] + get(got)).astype(BF16)


def act_join(place, a0, a1, a2, a3, out):
    for i, ref in enumerate((a0, a1, a2, a3)):
        j = place[1] ^ place[2] ^ i
        for z in range(4):
            for s in range(SEQS):
                at = pl.multiple_of((j * 4 + (place[3] ^ z)) * STEP, STEP)
                out[s, pl.ds(at, STEP), :] = ref[z * PIECE + s * STEP : z * PIECE + (s + 1) * STEP, :]


def square(place, acts, g, g_p, g_q, far_a, far_b, own, away):
    w, cols = g.shape[2], own.shape[1]
    for kind, far in enumerate((far_a, far_b)):
        total = None
        for s in range(SEQS):
            rows = []
            for ref in (g.at[kind], g_p.at[kind], far, g_q.at[kind]):
                for k in range(4):
                    at = k * PIECE + s * STEP
                    rows.append(ref[at : at + STEP, :])
            r = lax.dot_general(
                jnp.concatenate(rows, 0), acts[s], (((0,), (0,)), ((), ())), preferred_element_type=F32
            ) * F32(LEN**-0.5)
            total = r * r if total is None else total + r * r
        own[kind * w : (kind + 1) * w, :] = total[:, :cols]
        away[kind * w : (kind + 1) * w, :] = total[:, cols:]


def mean(place, *refs):
    out, parts = refs[-1], refs[:-1]
    rows = parts[0].shape[0]
    for i in range(len(parts) // 2):
        out[i * rows : (i + 1) * rows, :] = (parts[2 * i][...] + parts[2 * i + 1][...]) / F32(2 * SEQS)


def after(a, *others):
    return lax.optimization_barrier((a, *others))[0]


def shards(activations, out_grads, act_basis, grad_basis):
    row, col = lax.axis_index("row"), lax.axis_index("col")
    core = col % 2
    place = jnp.stack([core, row // 2, (col // 2) % 4, col // 8]).astype(jnp.int32)
    feats, dirs = grad_basis.shape
    cols = act_basis.shape[1]
    w = dirs // (2 * PAIRS)

    def columns(shape, index):
        return pl.BlockSpec(shape, lambda i, s: (0, index))

    def core_half(n):
        return pl.BlockSpec((HALF, n), lambda i, s: (s[0], 0))

    ab_got = col_swap(act_basis, core=1)
    og_got = col_swap(after(out_grads, ab_got), core=1)
    gb_got = col_swap(after(grad_basis, ab_got), core=1)

    a_shape = (QUARTER, 2 * cols)
    a_send = ((QUARTER + TAIL, 2 * cols), BF16)
    acts_feats = activations.shape[1]
    *a_sends, a_keep = call(
        act_first,
        place,
        [a_send] * 3 + [(a_shape, F32)],
        (activations, act_basis, ab_got),
        {0: core_half(acts_feats)},
        "act_first",
        2 * HALF * acts_feats * 2 * cols,
    )
    a_got = [row_swap(a, x=k) for k, a in zip((1, 2, 3), a_sends)]

    grad_ins = (out_grads, og_got, grad_basis, gb_got)
    grad_specs = {0: core_half(feats), 1: core_half(feats)}
    grad_flops = 2 * QUARTER * 2 * feats * dirs
    send_a, send_b = call(
        grad_first,
        after(place, a_keep),
        [((QUARTER + TAIL, dirs // 2), BF16)] * 2,
        grad_ins,
        grad_specs,
        "grad_first",
        grad_flops,
    )
    got_a, got_b = col_swap(send_a, y=3), col_swap(send_b, y=1)

    p1, p3, p0 = call(
        grad_rest,
        after(place, send_a),
        [((QUARTER, dirs), F32)] * 3,
        grad_ins,
        grad_specs,
        "grad_rest",
        3 * grad_flops,
    )

    got_p, got_q = [], []
    token = p0
    for pair in range(PAIRS):
        wide, narrow = columns((QUARTER, 2 * w), pair), columns((QUARTER + TAIL, w), pair)
        send_p, send_q = call(
            grad_second,
            after(place, token),
            [((QUARTER + TAIL, 2 * w), BF16)] * 2,
            (p1, p3, got_a, got_b),
            {0: wide, 1: wide, 2: narrow, 3: narrow},
            f"grad_second{pair}",
        )
        token = send_p
        got_p.append(col_swap(send_p, y=1))
        got_q.append(col_swap(send_q, y=3))

    a_send2, a_total = call(
        act_second, after(place, token), [a_send, (a_shape, F32)], (a_keep, *a_got), None, "act_second"
    )
    a_got2 = row_swap(a_send2, z=1)
    token = a_total

    keeps, z_gots = [], []
    for pair in range(PAIRS):
        *z_sends, keep = call(
            grad_z,
            after(place, token),
            [((PIECE + TAIL, 2 * w), BF16)] * 3 + [((PIECE, 2 * w), F32)],
            (p0, got_p[pair], got_q[pair]),
            {0: columns((QUARTER, 2 * w), pair)},
            f"grad_z{pair}",
        )
        token = keep
        keeps.append(keep)
        z_gots.append([col_swap(a, z=k) for k, a in zip((1, 2, 3), z_sends)])

    g_all = []
    for pair in range(PAIRS):
        (g_own,) = call(
            grad_round,
            after(place, token),
            [((PIECE, 2 * w), BF16)],
            (keeps[pair], *z_gots[pair]),
            None,
            f"grad_round{pair}",
        )
        token = g_own
        g_all.append([g_own, *[col_swap(g_own, z=k) for k in (1, 2, 3)]])
        if pair == 0:
            (a_own,) = call(
                act_round, after(place, token), [(a_shape, BF16)], (a_total, a_got2), None, "act_round"
            )
            token = a_own
            a_all = [a_own, *[row_swap(a_own, x=k) for k in (1, 2, 3)]]

    gs = []
    for pair in range(PAIRS):
        (g,) = call(
            grad_join, after(place, token), [((2, QUARTER, w), BF16)], g_all[pair], None, f"grad_join{pair}"
        )
        token = g
        gs.append((g, col_swap(g, y=1), col_swap(g, y=3)))
        if pair == 0:
            (acts,) = call(
                act_join, after(place, token), [((SEQS, LEN, 2 * cols), BF16)], a_all, None, "act_join"
            )
            token = acts

    parts = []
    for pair in range(PAIRS):
        g, g_p, g_q = gs[pair]
        far_a, far_b = col_swap(g_p[0], y=3), col_swap(g_q[1], y=1)
        own, away = call(
            square,
            place,
            [((2 * w, cols), F32)] * 2,
            (acts, g, g_p, g_q, far_a, far_b),
            None,
            f"square{pair}",
            2 * HALF * 2 * w * 2 * cols,
        )
        parts += [own, col_swap(away, core=1)]
    (out,) = call(mean, place, [((dirs, cols), F32)], parts, None, "mean")
    return out


def solution(mesh):
    return jax.shard_map(
        shards,
        mesh=mesh,
        in_specs=(P(None, "row"), P(None, "col"), P("row", "col"), P("col", "row")),
        out_specs=P("row", "col"),
        check_vma=False,
    )
```

```python
import functools

import jax
import jax.numpy as jnp
from jax import lax
from jax.experimental import pallas as pl
from jax.experimental.pallas import tpu as pltpu
from jax.sharding import PartitionSpec as P

LEN = 512
SEQS, HALF, QUARTER, PIECE, STEP = 3, 1536, 384, 96, 32
TAIL = 16
PAIRS = 2
F32, BF16 = jnp.float32, jnp.bfloat16


def col_swap(a, y=0, z=0, core=0):
    perm = [(i, i ^ (z * 8 + y * 2 + core)) for i in range(32)]
    return lax.ppermute(a, "col", perm)


def row_swap(a, x=0, z=0):
    perm = [(i, i ^ (x * 2 + z)) for i in range(8)]
    return lax.ppermute(a, "row", perm)


def exponent(v):
    return jnp.maximum(jnp.floor(jnp.log2(jnp.max(jnp.abs(v), keepdims=True))) + 2.0, -100.0)


def put(ref, v):
    rows = v.shape[0]
    e = exponent(v)
    t = v * jnp.exp2(16.0 - e)
    t = t * t
    t = t * t
    t = t * t
    ref[0:rows, :] = jnp.where(v < 0, -t, t).astype(BF16)
    ref[rows : rows + TAIL, :] = jnp.broadcast_to(e, (TAIL, ref.shape[1])).astype(BF16)


def get(ref, rows=None):
    end = ref.shape[0]
    e = ref[end - TAIL : end, :][0:1, 0:1].astype(F32)
    c = ref[slice(0, end - TAIL) if rows is None else rows, :].astype(F32)
    t = jnp.exp2(jnp.log2(jnp.abs(c)) * 0.125 + (e - 16.0))
    return jnp.where(c < 0, -t, t)


def quarter_rows(ref, q):
    rows = []
    for z in range(4):
        for s in range(SEQS):
            at = pl.multiple_of(s * LEN + q * (4 * STEP) + z * STEP, STEP)
            rows.append(ref[pl.ds(at, STEP), :])
    return jnp.concatenate(rows, 0)


def call(body, place, outs, ins, specs=None, name=None, flops=0):
    specs = specs or {}

    def whole(shape):
        return pl.BlockSpec(shape, lambda i, s: (0,) * len(shape))

    nbytes = sum(a.size * a.dtype.itemsize for a in ins) + sum(
        functools.reduce(lambda a, b: a * b, s, 1) * jnp.dtype(d).itemsize for s, d in outs
    )
    return pl.pallas_call(
        body,
        out_shape=[jax.ShapeDtypeStruct(s, d) for s, d in outs],
        grid_spec=pltpu.PrefetchScalarGridSpec(
            num_scalar_prefetch=1,
            grid=(1,),
            in_specs=[specs.get(i) or whole(a.shape) for i, a in enumerate(ins)],
            out_specs=[whole(s) for s, _ in outs],
        ),
        compiler_params=pltpu.CompilerParams(vmem_limit_bytes=24 * 2**20),
        cost_estimate=pl.CostEstimate(flops=flops, bytes_accessed=nbytes, transcendentals=0),
        name=name,
    )(place, *ins)


def grad_dot(own, got, gb_own, gb_got, q):
    p = jnp.dot(quarter_rows(own, q), gb_own[...], preferred_element_type=F32)
    return p + jnp.dot(quarter_rows(got, q), gb_got[...], preferred_element_type=F32)


def grad_first(place, own, got, gb_own, gb_got, send_a, send_b):
    p = grad_dot(own, got, gb_own, gb_got, place[2] ^ 2)
    w = p.shape[1] // (2 * PAIRS)
    for kind, ref in enumerate((send_a, send_b)):
        put(ref, jnp.concatenate([p[:, (2 * i + kind) * w : (2 * i + kind + 1) * w] for i in range(PAIRS)], 1))


def grad_rest(place, own, got, gb_own, gb_got, p1, p3, p0):
    for j, ref in ((1, p1), (3, p3), (0, p0)):
        ref[...] = grad_dot(own, got, gb_own, gb_got, place[2] ^ j)


def grad_second(place, p1, p3, got_a, got_b, send_p, send_q):
    w = got_a.shape[1]
    put(send_p, jnp.concatenate([p1[:, :w] + get(got_a), p1[:, w:]], 1))
    put(send_q, jnp.concatenate([p3[:, :w], p3[:, w:] + get(got_b)], 1))


def grad_z(place, p0, got_p, got_q, send1, send2, send3, keep):
    for k, ref in ((1, send1), (2, send2), (3, send3), (0, keep)):
        rows = pl.ds(pl.multiple_of((place[3] ^ k) * PIECE, STEP), PIECE)
        v = p0[rows, :] + get(got_p, rows) + get(got_q, rows)
        if k:
            put(ref, v)
        else:
            ref[...] = v


def grad_round(place, own, got1, got2, got3, out):
    out[...] = (own[...] + get(got1) + get(got2) + get(got3)).astype(BF16)


def grad_join(place, g0, g1, g2, g3, out):
    w = out.shape[2]
    for k, ref in enumerate((g0, g1, g2, g3)):
        for kind in range(2):
            out[kind, k * PIECE : (k + 1) * PIECE, :] = ref[:, kind * w : (kind + 1) * w]


def act_first(place, acts, ab_own, ab_got, send_a, send_b, keep0, keep1, keep3):
    w = ab_own.shape[1]
    for k, ref in ((2, None), (1, keep1), (3, keep3), (0, keep0)):
        rows = quarter_rows(acts, place[1] ^ k)
        v = jnp.concatenate([jnp.dot(rows, ab[...], preferred_element_type=F32) for ab in (ab_own, ab_got)], 1)
        if k == 2:
            put(send_a, v[:, :w])
            put(send_b, v[:, w:])
        else:
            ref[...] = v


def act_mid(place, keep1, keep3, got_a, got_b, send_p, send_q):
    w = got_a.shape[1]
    put(send_p, jnp.concatenate([keep1[:, :w] + get(got_a), keep1[:, w:]], 1))
    put(send_q, jnp.concatenate([keep3[:, :w], keep3[:, w:] + get(got_b)], 1))


def act_second(place, keep, got_p, got_q, total, *sends):
    v = keep[...] + get(got_p) + get(got_q)
    total[...] = v
    w = sends[0].shape[1]
    for i, ref in enumerate(sends):
        put(ref, v[:, i * w : (i + 1) * w])


def act_round(place, total, *refs):
    out, gots = refs[-1], refs[:-1]
    w = gots[0].shape[1]
    for i, got in enumerate(gots):
        out[:, i * w : (i + 1) * w] = (total[:, i * w : (i + 1) * w] + get(got)).astype(BF16)


def act_join(place, a0, a1, a2, a3, out):
    for i, ref in enumerate((a0, a1, a2, a3)):
        j = place[1] ^ place[2] ^ i
        for z in range(4):
            for s in range(SEQS):
                at = pl.multiple_of((j * 4 + (place[3] ^ z)) * STEP, STEP)
                out[s, pl.ds(at, STEP), :] = ref[z * PIECE + s * STEP : z * PIECE + (s + 1) * STEP, :]


def square(place, acts, g, g_p, g_q, far_a, far_b, own, away):
    w, cols = g.shape[2], own.shape[1]
    for kind, far in enumerate((far_a, far_b)):
        total = None
        for s in range(SEQS):
            rows = []
            for ref in (g.at[kind], g_p.at[kind], far, g_q.at[kind]):
                for k in range(4):
                    at = k * PIECE + s * STEP
                    rows.append(ref[at : at + STEP, :])
            r = lax.dot_general(
                jnp.concatenate(rows, 0), acts[s], (((0,), (0,)), ((), ())), preferred_element_type=F32
            ) * F32(LEN**-0.5)
            total = r * r if total is None else total + r * r
        own[kind * w : (kind + 1) * w, :] = total[:, :cols]
        away[kind * w : (kind + 1) * w, :] = total[:, cols:]


def mean(place, *refs):
    out, parts = refs[-1], refs[:-1]
    rows = parts[0].shape[0]
    for i in range(len(parts) // 2):
        out[i * rows : (i + 1) * rows, :] = (parts[2 * i][...] + parts[2 * i + 1][...]) / F32(2 * SEQS)


def after(a, *others):
    return lax.optimization_barrier((a, *others))[0]


def shards(activations, out_grads, act_basis, grad_basis):
    row, col = lax.axis_index("row"), lax.axis_index("col")
    core = col % 2
    place = jnp.stack([core, row // 2, (col // 2) % 4, col // 8]).astype(jnp.int32)
    feats, dirs = grad_basis.shape
    cols = act_basis.shape[1]
    w = dirs // (2 * PAIRS)

    def columns(shape, index):
        return pl.BlockSpec(shape, lambda i, s: (0, index))

    def core_half(n):
        return pl.BlockSpec((HALF, n), lambda i, s: (s[0], 0))

    ab_got = col_swap(act_basis, core=1)
    og_got = col_swap(after(out_grads, ab_got), core=1)
    gb_got = col_swap(after(grad_basis, ab_got), core=1)

    a_shape = (QUARTER, 2 * cols)
    a_send = ((QUARTER + TAIL, 2 * cols), BF16)
    acts_feats = activations.shape[1]
    send_a, send_b, a_keep, a_keep1, a_keep3 = call(
        act_first,
        place,
        [((QUARTER + TAIL, cols), BF16)] * 2 + [(a_shape, F32)] * 3,
        (activations, act_basis, ab_got),
        {0: core_half(acts_feats)},
        "act_first",
        2 * HALF * acts_feats * 2 * cols,
    )
    a_got_a, a_got_b = row_swap(send_a, x=3), row_swap(send_b, x=1)

    grad_ins = (out_grads, og_got, grad_basis, gb_got)
    grad_specs = {0: core_half(feats), 1: core_half(feats)}
    grad_flops = 2 * QUARTER * 2 * feats * dirs
    send_a, send_b = call(
        grad_first,
        after(place, a_keep),
        [((QUARTER + TAIL, dirs // 2), BF16)] * 2,
        grad_ins,
        grad_specs,
        "grad_first",
        grad_flops,
    )
    got_a, got_b = col_swap(send_a, y=3), col_swap(send_b, y=1)

    p1, p3, p0 = call(
        grad_rest,
        after(place, send_a),
        [((QUARTER, dirs), F32)] * 3,
        grad_ins,
        grad_specs,
        "grad_rest",
        3 * grad_flops,
    )

    send_p, send_q = call(
        act_mid, after(place, p1), [a_send] * 2, (a_keep1, a_keep3, a_got_a, a_got_b), None, "act_mid"
    )
    a_got_p, a_got_q = row_swap(send_p, x=1), row_swap(send_q, x=3)

    got_p, got_q = [], []
    token = send_p
    for pair in range(PAIRS):
        wide, narrow = columns((QUARTER, 2 * w), pair), columns((QUARTER + TAIL, w), pair)
        send_p, send_q = call(
            grad_second,
            after(place, token),
            [((QUARTER + TAIL, 2 * w), BF16)] * 2,
            (p1, p3, got_a, got_b),
            {0: wide, 1: wide, 2: narrow, 3: narrow},
            f"grad_second{pair}",
        )
        token = send_p
        got_p.append(col_swap(send_p, y=1))
        got_q.append(col_swap(send_q, y=3))

    a_total, *sends = call(
        act_second,
        after(place, token),
        [(a_shape, F32)] + [((QUARTER + TAIL, cols), BF16)] * 2,
        (a_keep, a_got_p, a_got_q),
        None,
        "act_second",
    )
    a_got2 = [row_swap(a, z=1) for a in sends]
    token = a_total

    keeps, z_gots = [], []
    for pair in range(PAIRS):
        *z_sends, keep = call(
            grad_z,
            after(place, token),
            [((PIECE + TAIL, 2 * w), BF16)] * 3 + [((PIECE, 2 * w), F32)],
            (p0, got_p[pair], got_q[pair]),
            {0: columns((QUARTER, 2 * w), pair)},
            f"grad_z{pair}",
        )
        token = keep
        keeps.append(keep)
        z_gots.append([col_swap(a, z=k) for k, a in zip((1, 2, 3), z_sends)])

    g_all = []
    for pair in range(PAIRS):
        (g_own,) = call(
            grad_round,
            after(place, token),
            [((PIECE, 2 * w), BF16)],
            (keeps[pair], *z_gots[pair]),
            None,
            f"grad_round{pair}",
        )
        token = g_own
        g_all.append([g_own, *[col_swap(g_own, z=k) for k in (1, 2, 3)]])
        if pair == 0:
            (a_own,) = call(
                act_round, after(place, token), [(a_shape, BF16)], (a_total, *a_got2), None, "act_round"
            )
            token = a_own
            a_all = [a_own, *[row_swap(a_own, x=k) for k in (1, 2, 3)]]

    gs = []
    for pair in range(PAIRS):
        (g,) = call(
            grad_join, after(place, token), [((2, QUARTER, w), BF16)], g_all[pair], None, f"grad_join{pair}"
        )
        token = g
        gs.append((g, col_swap(g, y=1), col_swap(g, y=3)))
        if pair == 0:
            (acts,) = call(
                act_join, after(place, token), [((SEQS, LEN, 2 * cols), BF16)], a_all, None, "act_join"
            )
            token = acts

    parts = []
    for pair in range(PAIRS):
        g, g_p, g_q = gs[pair]
        far_a, far_b = col_swap(g_p[0], y=3), col_swap(g_q[1], y=1)
        own, away = call(
            square,
            place,
            [((2 * w, cols), F32)] * 2,
            (acts, g, g_p, g_q, far_a, far_b),
            None,
            f"square{pair}",
            2 * HALF * 2 * w * 2 * cols,
        )
        parts += [own, col_swap(away, core=1)]
    (out,) = call(mean, place, [((dirs, cols), F32)], parts, None, "mean")
    return out


def solution(mesh):
    return jax.shard_map(
        shards,
        mesh=mesh,
        in_specs=(P(None, "row"), P(None, "col"), P("row", "col"), P("col", "row")),
        out_specs=P("row", "col"),
        check_vma=False,
    )
```

```python
import functools

import jax
import jax.numpy as jnp
from jax import lax
from jax.experimental import pallas as pl
from jax.experimental.pallas import tpu as pltpu
from jax.sharding import PartitionSpec as P

LEN = 512
SEQS, HALF, QUARTER, PIECE, STEP = 3, 1536, 384, 96, 32
TAIL = 16
PAIRS = 2
F32, BF16 = jnp.float32, jnp.bfloat16


def col_swap(a, y=0, z=0, core=0):
    perm = [(i, i ^ (z * 8 + y * 2 + core)) for i in range(32)]
    return lax.ppermute(a, "col", perm)


def row_swap(a, x=0, z=0):
    perm = [(i, i ^ (x * 2 + z)) for i in range(8)]
    return lax.ppermute(a, "row", perm)


def exponent(v):
    return jnp.maximum(jnp.floor(jnp.log2(jnp.max(jnp.abs(v), keepdims=True))) + 2.0, -100.0)


def put(ref, v):
    rows = v.shape[0]
    e = exponent(v)
    t = v * jnp.exp2(16.0 - e)
    t = t * t
    t = t * t
    t = t * t
    ref[0:rows, :] = jnp.where(v < 0, -t, t).astype(BF16)
    ref[rows : rows + TAIL, :] = jnp.broadcast_to(e, (TAIL, ref.shape[1])).astype(BF16)


def get(ref, rows=None):
    end = ref.shape[0]
    e = ref[end - TAIL : end, :][0:1, 0:1].astype(F32)
    c = ref[slice(0, end - TAIL) if rows is None else rows, :].astype(F32)
    t = jnp.exp2(jnp.log2(jnp.abs(c)) * 0.125 + (e - 16.0))
    return jnp.where(c < 0, -t, t)


def quarter_rows(ref, q):
    rows = []
    for z in range(4):
        for s in range(SEQS):
            at = pl.multiple_of(s * LEN + q * (4 * STEP) + z * STEP, STEP)
            rows.append(ref[pl.ds(at, STEP), :])
    return jnp.concatenate(rows, 0)


def call(body, place, outs, ins, specs=None, name=None, flops=0):
    specs = specs or {}

    def whole(shape):
        return pl.BlockSpec(shape, lambda i, s: (0,) * len(shape))

    nbytes = sum(a.size * a.dtype.itemsize for a in ins) + sum(
        functools.reduce(lambda a, b: a * b, s, 1) * jnp.dtype(d).itemsize for s, d in outs
    )
    return pl.pallas_call(
        body,
        out_shape=[jax.ShapeDtypeStruct(s, d) for s, d in outs],
        grid_spec=pltpu.PrefetchScalarGridSpec(
            num_scalar_prefetch=1,
            grid=(1,),
            in_specs=[specs.get(i) or whole(a.shape) for i, a in enumerate(ins)],
            out_specs=[whole(s) for s, _ in outs],
        ),
        compiler_params=pltpu.CompilerParams(vmem_limit_bytes=24 * 2**20),
        cost_estimate=pl.CostEstimate(flops=flops, bytes_accessed=nbytes, transcendentals=0),
        name=name,
    )(place, *ins)


def grad_dot(own, got, gb_own, gb_got, q):
    p = jnp.dot(quarter_rows(own, q), gb_own[...], preferred_element_type=F32)
    return p + jnp.dot(quarter_rows(got, q), gb_got[...], preferred_element_type=F32)


def grad_first(place, own, got, gb_own, gb_got, send_a, send_b):
    p = grad_dot(own, got, gb_own, gb_got, place[2] ^ 2)
    w = p.shape[1] // (2 * PAIRS)
    for kind, ref in enumerate((send_a, send_b)):
        put(ref, jnp.concatenate([p[:, (2 * i + kind) * w : (2 * i + kind + 1) * w] for i in range(PAIRS)], 1))


def grad_rest(place, own, got, gb_own, gb_got, p1, p3, p0):
    for j, ref in ((1, p1), (3, p3), (0, p0)):
        ref[...] = grad_dot(own, got, gb_own, gb_got, place[2] ^ j)


def grad_second(place, p1, p3, got_a, got_b, send_p, send_q):
    w = got_a.shape[1]
    put(send_p, jnp.concatenate([p1[:, :w] + get(got_a), p1[:, w:]], 1))
    put(send_q, jnp.concatenate([p3[:, :w], p3[:, w:] + get(got_b)], 1))


def grad_z(place, p0, got_p, got_q, send1, send2, send3, keep):
    for k, ref in ((1, send1), (2, send2), (3, send3), (0, keep)):
        rows = pl.ds(pl.multiple_of((place[3] ^ k) * PIECE, STEP), PIECE)
        v = p0[rows, :] + get(got_p, rows) + get(got_q, rows)
        if k:
            put(ref, v)
        else:
            ref[...] = v


def grad_round(place, own, got1, got2, got3, out):
    out[...] = (own[...] + get(got1) + get(got2) + get(got3)).astype(BF16)


def grad_join(place, g0, g1, g2, g3, out):
    w = out.shape[2]
    for k, ref in enumerate((g0, g1, g2, g3)):
        for kind in range(2):
            out[kind, k * PIECE : (k + 1) * PIECE, :] = ref[:, kind * w : (kind + 1) * w]


def act_first(place, acts, ab_own, ab_got, send_a, send_b, keep0, keep1, keep3):
    w = ab_own.shape[1]
    for k, ref in ((2, None), (1, keep1), (3, keep3), (0, keep0)):
        rows = quarter_rows(acts, place[1] ^ k)
        v = jnp.concatenate([jnp.dot(rows, ab[...], preferred_element_type=F32) for ab in (ab_own, ab_got)], 1)
        if k == 2:
            put(send_a, v[:, :w])
            put(send_b, v[:, w:])
        else:
            ref[...] = v


def act_mid(place, keep1, keep3, got_a, got_b, send_p, send_q):
    w = got_a.shape[1]
    put(send_p, jnp.concatenate([keep1[:, :w] + get(got_a), keep1[:, w:]], 1))
    put(send_q, jnp.concatenate([keep3[:, :w], keep3[:, w:] + get(got_b)], 1))


def act_second(place, keep, got_p, got_q, total, *sends):
    v = keep[...] + get(got_p) + get(got_q)
    total[...] = v
    w = sends[0].shape[1]
    for i, ref in enumerate(sends):
        put(ref, v[:, i * w : (i + 1) * w])


def act_round(place, total, *refs):
    out, gots = refs[-1], refs[:-1]
    w = gots[0].shape[1]
    for i, got in enumerate(gots):
        out[:, i * w : (i + 1) * w] = (total[:, i * w : (i + 1) * w] + get(got)).astype(BF16)


def act_join(place, a0, a1, a2, a3, out):
    for i, ref in enumerate((a0, a1, a2, a3)):
        j = place[1] ^ place[2] ^ i
        for z in range(4):
            for s in range(SEQS):
                at = pl.multiple_of((j * 4 + (place[3] ^ z)) * STEP, STEP)
                out[s, pl.ds(at, STEP), :] = ref[z * PIECE + s * STEP : z * PIECE + (s + 1) * STEP, :]


def square(place, acts, g, g_p, g_q, far_a, far_b, own, away):
    w, cols = g.shape[2], own.shape[1]
    for kind, far in enumerate((far_a, far_b)):
        total = None
        for s in range(SEQS):
            rows = []
            for ref in (g.at[kind], g_p.at[kind], far, g_q.at[kind]):
                for k in range(4):
                    at = k * PIECE + s * STEP
                    rows.append(ref[at : at + STEP, :])
            r = lax.dot_general(
                jnp.concatenate(rows, 0), acts[s], (((0,), (0,)), ((), ())), preferred_element_type=F32
            ) * F32(LEN**-0.5)
            total = r * r if total is None else total + r * r
        own[kind * w : (kind + 1) * w, :] = total[:, :cols]
        away[kind * w : (kind + 1) * w, :] = total[:, cols:]


def mean(place, *refs):
    out, parts = refs[-1], refs[:-1]
    rows = parts[0].shape[0]
    for i in range(len(parts) // 2):
        out[i * rows : (i + 1) * rows, :] = (parts[2 * i][...] + parts[2 * i + 1][...]) / F32(2 * SEQS)


def after(a, *others):
    return lax.optimization_barrier((a, *others))[0]


def shards(activations, out_grads, act_basis, grad_basis):
    row, col = lax.axis_index("row"), lax.axis_index("col")
    core = col % 2
    place = jnp.stack([core, row // 2, (col // 2) % 4, col // 8]).astype(jnp.int32)
    feats, dirs = grad_basis.shape
    cols = act_basis.shape[1]
    w = dirs // (2 * PAIRS)

    def columns(shape, index):
        return pl.BlockSpec(shape, lambda i, s: (0, index))

    def core_half(n):
        return pl.BlockSpec((HALF, n), lambda i, s: (s[0], 0))

    ab_got = col_swap(act_basis, core=1)
    og_got = col_swap(after(out_grads, ab_got), core=1)
    gb_got = col_swap(after(grad_basis, ab_got), core=1)

    a_shape = (QUARTER, 2 * cols)
    a_send = ((QUARTER + TAIL, 2 * cols), BF16)
    acts_feats = activations.shape[1]
    send_a, send_b, a_keep, a_keep1, a_keep3 = call(
        act_first,
        place,
        [((QUARTER + TAIL, cols), BF16)] * 2 + [(a_shape, F32)] * 3,
        (activations, act_basis, ab_got),
        {0: core_half(acts_feats)},
        "act_first",
        2 * HALF * acts_feats * 2 * cols,
    )
    a_got_a, a_got_b = row_swap(send_a, x=3), row_swap(send_b, x=1)

    grad_ins = (out_grads, og_got, grad_basis, gb_got)
    grad_specs = {0: core_half(feats), 1: core_half(feats)}
    grad_flops = 2 * QUARTER * 2 * feats * dirs
    send_a, send_b = call(
        grad_first,
        after(place, a_keep),
        [((QUARTER + TAIL, dirs // 2), BF16)] * 2,
        grad_ins,
        grad_specs,
        "grad_first",
        grad_flops,
    )
    got_a, got_b = col_swap(send_a, y=3), col_swap(send_b, y=1)

    p1, p3, p0 = call(
        grad_rest,
        after(place, send_a),
        [((QUARTER, dirs), F32)] * 3,
        grad_ins,
        grad_specs,
        "grad_rest",
        3 * grad_flops,
    )

    send_p, send_q = call(
        act_mid, after(place, p1), [a_send] * 2, (a_keep1, a_keep3, a_got_a, a_got_b), None, "act_mid"
    )
    a_got_p, a_got_q = row_swap(send_p, x=1), row_swap(send_q, x=3)

    got_p, got_q = [], []
    token = send_p
    for pair in range(PAIRS):
        wide, narrow = columns((QUARTER, 2 * w), pair), columns((QUARTER + TAIL, w), pair)
        send_p, send_q = call(
            grad_second,
            after(place, token),
            [((QUARTER + TAIL, 2 * w), BF16)] * 2,
            (p1, p3, got_a, got_b),
            {0: wide, 1: wide, 2: narrow, 3: narrow},
            f"grad_second{pair}",
        )
        token = send_p
        got_p.append(col_swap(send_p, y=1))
        got_q.append(col_swap(send_q, y=3))

    a_total, *sends = call(
        act_second,
        after(place, token),
        [(a_shape, F32)] + [((QUARTER + TAIL, cols), BF16)] * 2,
        (a_keep, a_got_p, a_got_q),
        None,
        "act_second",
    )
    a_got2 = [row_swap(a, z=1) for a in sends]
    token = a_total

    keeps, z_gots = [], []
    for pair in range(PAIRS):
        *z_sends, keep = call(
            grad_z,
            after(place, token),
            [((PIECE + TAIL, 2 * w), BF16)] * 3 + [((PIECE, 2 * w), F32)],
            (p0, got_p[pair], got_q[pair]),
            {0: columns((QUARTER, 2 * w), pair)},
            f"grad_z{pair}",
        )
        token = keep
        keeps.append(keep)
        z_gots.append([col_swap(a, z=k) for k, a in zip((1, 2, 3), z_sends)])

    g_all = []
    for pair in range(PAIRS):
        (g_own,) = call(
            grad_round,
            after(place, token),
            [((PIECE, 2 * w), BF16)],
            (keeps[pair], *z_gots[pair]),
            None,
            f"grad_round{pair}",
        )
        token = g_own
        g_all.append([g_own, *[col_swap(g_own, z=k) for k in (3, 2, 1)][::-1]])
        if pair == 0:
            (a_own,) = call(
                act_round, after(place, token), [(a_shape, BF16)], (a_total, *a_got2), None, "act_round"
            )
            token = a_own
            a_all = [a_own, *[row_swap(a_own, x=k) for k in (1, 2, 3)]]

    gs = []
    for pair in range(PAIRS):
        (g,) = call(
            grad_join, after(place, token), [((2, QUARTER, w), BF16)], g_all[pair], None, f"grad_join{pair}"
        )
        token = g
        gs.append((g, col_swap(g, y=1), col_swap(g, y=3)))
        if pair == 0:
            (acts,) = call(
                act_join, after(place, token), [((SEQS, LEN, 2 * cols), BF16)], a_all, None, "act_join"
            )
            token = acts

    parts = []
    for pair in range(PAIRS):
        g, g_p, g_q = gs[pair]
        far_a, far_b = col_swap(g_p[0], y=3), col_swap(g_q[1], y=1)
        own, away = call(
            square,
            place,
            [((2 * w, cols), F32)] * 2,
            (acts, g, g_p, g_q, far_a, far_b),
            None,
            f"square{pair}",
            2 * HALF * 2 * w * 2 * cols,
        )
        parts += [own, col_swap(away, core=1)]
    (out,) = call(mean, place, [((dirs, cols), F32)], parts, None, "mean")
    return out


def solution(mesh):
    return jax.shard_map(
        shards,
        mesh=mesh,
        in_specs=(P(None, "row"), P(None, "col"), P("row", "col"), P("col", "row")),
        out_specs=P("row", "col"),
        check_vma=False,
    )
```
